512 devices in a mesh: plane: 64 (over z, x_lo, core), tower: 8 (over x_hi, y).
Axes of the slice: x: 4 (x_hi: 2, x_lo: 2; x = x_hi * 2 + x_lo), y: 4, z: 16, core: 2. Of those that a mesh axis runs over, the one named last changes fastest.
Arguments:
- offsets: bfloat16 [64, 16, 3, 128], P('plane', 'tower'), may hold values from 0 to 1, as said below
- features: bfloat16 [64, 16, 128, 256], P('plane', 'tower'), may hold values from -6 to 6
- cotangent: bfloat16 [64, 16, 128, 256], P('plane', 'tower'), may hold values from -6 to 6
- w_in: bfloat16 [256, 256], replicated, may hold values from -0.375 to 0.375
- w_out: bfloat16 [256, 256], replicated, may hold values from -0.375 to 0.375
- w_filter: bfloat16 [8, 256], replicated, may hold values from -2 to 2
- counts: int32 [64, 16], P('plane', 'tower'), may hold values from 64 to 128
Outputs:
- forces: float32 [64, 16, 3, 128], P('plane', 'tower')
The draws below stay inside these ranges and needn't reach their ends.
Inputs may be any that keep to these rules, and one draw needn't show every extreme that they name: offsets lie in the unit box.
All inputs are finite; a program needn't handle non-finite values.
Results may differ from the reference program's by a relative error of at most 0.005.
Values may be sent and summed in bfloat16 or wider, within the bound.
No kernel may reach another device: no remote copies, remote signals or barrier semaphores. Data moves between devices by JAX's collectives and lax.ppermute only.
A program may use at most 64 MiB of HBM per device.

```python
import jax
import jax.numpy as jnp
from jax import lax

F = 256
RADIAL = 8
BOX = 128
PLANE_BOXES = 64
COLUMN = 16


def draw_offsets(key, part):
    key = jax.random.fold_in(key, 11)
    key_base, key_pick = jax.random.split(key)
    base = jax.random.uniform(key_base, (PLANE_BOXES, COLUMN, 3, BOX), jnp.float32, 0.0, 1.0)
    picked = jax.random.randint(key_pick, (PLANE_BOXES,), 0, COLUMN)
    chosen = jnp.arange(COLUMN, dtype=jnp.int32)[None, :] == picked[:, None]
    squeeze = jnp.where(chosen, 0.35, 1.0).astype(jnp.float32)
    planar = jnp.array([1.0, 1.0, 0.0], dtype=jnp.float32)
    factor = 1.0 - (1.0 - squeeze)[:, :, None, None] * planar[None, None, :, None]
    return (base * factor).astype(jnp.bfloat16)


def plant(values, own_key, least, high):
    index_at = [jax.random.randint(jax.random.fold_in(own_key, axis), (), 0, length) for axis, length in enumerate(values.shape)]
    main_axis = values.shape.index(max(values.shape))
    neighbour = index_at[:main_axis] + [(index_at[main_axis] + 1) % values.shape[main_axis]] + index_at[main_axis + 1:]
    return values.at[tuple(index_at)].set(least).at[tuple(neighbour)].set(high)


def levels(rng, extent, cuts, low, top_value):
    gain = 1.0
    for dim, shards_of in cuts:
        draws = jax.random.uniform(jax.random.fold_in(jax.random.fold_in(rng, 6), dim), (shards_of,), jnp.float32, low / len(cuts), top_value / len(cuts))
        gain = gain * jnp.repeat(jnp.exp(draws), extent[dim] // shards_of).reshape((-1,) + (1,) * (len(extent) - 1 - dim))
    return gain


def bell_draw(own_key, dims, width, most, shards=(), held_as=jnp.bfloat16):
    factor_of = levels(own_key, dims, shards, -0.22, 0.18) if shards else 1.0
    values = jax.random.normal(own_key, dims, jnp.float32) * width * factor_of
    return jnp.minimum(jnp.maximum(values, -most), most).astype(held_as)


def setup_inputs(seed: int = 0) -> dict:
    key_list = jax.random.split(jax.random.key(seed), 8)
    offsets = draw_offsets(jax.random.fold_in(key_list[7], 71), 0)
    features = bell_draw(key_list[1], (PLANE_BOXES, COLUMN, BOX, F), 1.0, 6.0, ((0, 64), (1, 8)))
    cotangent = bell_draw(key_list[2], (PLANE_BOXES, COLUMN, BOX, F), 1.0, 6.0, ((0, 64), (1, 8)))
    w_in = bell_draw(key_list[3], (F, F), F ** -0.5, 0.375)
    w_out = bell_draw(key_list[4], (F, F), F ** -0.5, 0.375)
    w_filter = bell_draw(key_list[5], (RADIAL, F), RADIAL ** -0.5, 2.0)
    counts = plant(jax.random.randint(key_list[6], (PLANE_BOXES, COLUMN), BOX // 2, BOX + 1), jax.random.fold_in(key_list[6], 1), BOX // 2, BOX).astype(jnp.int32)
    return {"offsets": offsets, "features": features, "cotangent": cotangent, "w_in": w_in, "w_out": w_out, "w_filter": w_filter, "counts": counts}


PITCH = 12.5
CUTOFF_SQUARED = 25.0
CENTER_STEP = 3.125
GAMMA = 0.2
FORCE_UNIT = 0.005


def reference(offsets, features, cotangent, w_in, w_out, w_filter, counts):
    planes = PLANE_BOXES
    column = COLUMN
    slots = jnp.arange(BOX, dtype=jnp.int32)
    live = (slots[None, None, :] < counts[:, :, None])[..., None]
    values = jnp.dot(features.reshape(-1, F), w_in, preferred_element_type=jnp.float32).reshape(planes, column, BOX, F)
    values = jnp.where(live, values, 0.0).astype(jnp.bfloat16)
    grads = lax.dot_general(cotangent.reshape(-1, F), w_out, (((1,), (1,)), ((), ())), preferred_element_type=jnp.float32)
    grads = jnp.where(live, grads.reshape(planes, column, BOX, F), 0.0).astype(jnp.bfloat16)
    units = offsets.astype(jnp.float32)
    centers = CENTER_STEP * jnp.arange(RADIAL).astype(jnp.float32)
    moves = [(across, upward) for across in (-1, 0, 1) for upward in (-1, 0, 1)]
    step_x = jnp.repeat(jnp.array([float(m[0]) for m in moves], dtype=jnp.float32), BOX)
    step_y = jnp.repeat(jnp.array([float(m[1]) for m in moves], dtype=jnp.float32), BOX)

    def visit(carry, position):
        plane_at = position // column
        box_at = position % column
        places = [((plane_at + planes + m[0]) % planes, (box_at + column + m[1]) % column) for m in moves]
        src_units = jnp.concatenate([units[p, b] for p, b in places], axis=1)
        src_values = jnp.concatenate([values[p, b] for p, b in places], axis=0)
        src_grads = jnp.concatenate([grads[p, b] for p, b in places], axis=0)
        own_units = units[plane_at, box_at]
        own_values = values[plane_at, box_at]
        own_grads = grads[plane_at, box_at]
        along_x = ((step_x[None, :] + src_units[0][None, :]) - own_units[0][:, None]) * PITCH
        along_y = ((step_y[None, :] + src_units[1][None, :]) - own_units[1][:, None]) * PITCH
        along_z = (src_units[2][None, :] - own_units[2][:, None]) * PITCH
        squared = along_x * along_x + along_y * along_y + along_z * along_z
        margin = jnp.maximum(1.0 - squared / CUTOFF_SQUARED, 0.0)
        spread = squared[:, None, :] - centers[None, :, None]
        decays = jnp.exp(-GAMMA * spread * spread)
        slopes = decays * (-2.0 * GAMMA * spread * (margin * margin)[:, None, :] - 2.0 * margin[:, None, :] / CUTOFF_SQUARED)
        filtered_own = (own_grads[:, None, :] * w_filter[None, :, :]).reshape(BOX * RADIAL, F)
        forward = lax.dot_general(filtered_own, src_values, (((1,), (1,)), ((), ())), preferred_element_type=jnp.float32)
        forward = forward.reshape(BOX, RADIAL, -1)
        filtered_src = (src_grads[:, None, :] * w_filter[None, :, :]).reshape(-1, F)
        backward = lax.dot_general(filtered_src, own_values, (((1,), (1,)), ((), ())), preferred_element_type=jnp.float32)
        backward = jnp.transpose(backward.reshape(-1, RADIAL, BOX), (2, 1, 0))
        strength = jnp.sum(slopes * (forward + backward), axis=1)
        force = 2.0 * FORCE_UNIT * jnp.stack([jnp.sum(strength * along_x, 1), jnp.sum(strength * along_y, 1), jnp.sum(strength * along_z, 1)])
        return carry, force

    _, forces = lax.scan(visit, jnp.zeros((), jnp.float32), jnp.arange(planes * column, dtype=jnp.int32))
    return forces.reshape(planes, column, 3, BOX)
```

```python
import math

import jax
import jax.numpy as jnp
from jax import lax
from jax.experimental import pallas as pl
from jax.experimental.pallas import tpu as pltpu
from jax.sharding import PartitionSpec as P

PITCH = 12.5
CUTOFF_SQUARED = 25.0
CENTER_STEP = 3.125
GAMMA = 0.2
FORCE_UNIT = 0.005
LOG2E = math.log2(math.e)

BOX = 128
F = 256
RADIAL = 8
MIDDLE = 4
ROWS = 16

STEPS = [math.exp(-GAMMA * CENTER_STEP**2 * (2 * m - 1)) for m in range(1, MIDDLE + 1)]


def vmem():
    return pl.BlockSpec(memory_space=pltpu.VMEM)


def smem():
    return pl.BlockSpec(memory_space=pltpu.SMEM)


def params(mib):
    return pltpu.CompilerParams(vmem_limit_bytes=mib * 2**20)


def packed_offsets(rows):
    tall = jnp.concatenate([rows, jnp.zeros((16 - rows.shape[0], BOX), jnp.float32)], axis=0)
    wide = jnp.concatenate([tall, jnp.zeros((16, 2 * F - BOX), jnp.float32)], axis=1)
    return wide.astype(jnp.bfloat16)


def prepare(odd_ref, counts_ref, offsets_ref, features_ref, cotangent_ref, w_in_ref, w_out_ref, own_ref, first_ref, second_ref):
    odd = odd_ref[0] == 1
    slots = lax.broadcasted_iota(jnp.int32, (BOX, F), 0)
    offsets = offsets_ref[...].astype(jnp.float32)
    boxes = []
    for b in range(2):
        live = slots < counts_ref[0, b]
        values = jnp.dot(features_ref[b], w_in_ref[...], preferred_element_type=jnp.float32)
        grads = lax.dot_general(
            cotangent_ref[b], w_out_ref[...], (((1,), (1,)), ((), ())), preferred_element_type=jnp.float32
        )
        both = jnp.concatenate([jnp.where(live, values, 0.0), jnp.where(live, grads, 0.0)], axis=1)
        boxes.append(both)
        own_ref[b * BOX : (b + 1) * BOX, :] = both.astype(jnp.bfloat16)
    own_ref[2 * BOX :, :] = packed_offsets(offsets.reshape(6, BOX))
    first_ref[:BOX, :] = jnp.where(odd, boxes[0], boxes[1]).astype(jnp.bfloat16)
    second_ref[:BOX, :] = jnp.where(odd, boxes[1], boxes[0]).astype(jnp.bfloat16)
    first_ref[BOX:, :] = packed_offsets(jnp.where(odd, offsets[:, 0], offsets[:, 1]))
    second_ref[BOX:, :] = packed_offsets(jnp.where(odd, offsets[:, 1], offsets[:, 0]))


def join(odd_ref, own_ref, first_ref, second_ref, column_ref):
    odd = odd_ref[0] == 1
    first = first_ref[...].astype(jnp.float32)
    second = second_ref[...].astype(jnp.float32)
    below = jnp.where(odd, first, second)
    above = jnp.where(odd, second, first)
    column_ref[:BOX, :] = below[:BOX].astype(jnp.bfloat16)
    column_ref[BOX : 3 * BOX, :] = own_ref[: 2 * BOX, :]
    column_ref[3 * BOX : 4 * BOX, :] = above[:BOX].astype(jnp.bfloat16)
    own = own_ref[2 * BOX :, :BOX].astype(jnp.float32)
    rows = []
    for c in range(3):
        rows += [below[BOX + c : BOX + c + 1, :BOX], own[2 * c : 2 * c + 2], above[BOX + c : BOX + c + 1, :BOX]]
    column_ref[4 * BOX :, :] = packed_offsets(jnp.concatenate(rows, axis=0))


def spread_weights(own_ref, w_filter_ref, out_ref):
    for b in range(2):
        values = own_ref[b * BOX : (b + 1) * BOX, :F].astype(jnp.float32)
        grads = own_ref[b * BOX : (b + 1) * BOX, F:].astype(jnp.float32)
        for k in range(RADIAL):
            w = w_filter_ref[k : k + 1, :].astype(jnp.float32)
            out_ref[b, k * BOX : (k + 1) * BOX, :F] = (grads * w).astype(jnp.bfloat16)
            out_ref[b, k * BOX : (k + 1) * BOX, F:] = (values * w).astype(jnp.bfloat16)


def strengths(dx, dy, dz, amplitudes):
    q = dx * dx + dy * dy + dz * dz
    c = jnp.maximum(1.0 - q * (1.0 / CUTOFF_SQUARED), 0.0)
    h = jnp.minimum(q, CUTOFF_SQUARED) - MIDDLE * CENTER_STEP
    middle = jnp.exp2(h * h * (-GAMMA * LOG2E))
    slope = 2.0 * GAMMA * CENTER_STEP * LOG2E
    up = jnp.exp2(h * slope)
    down = jnp.exp2(h * -slope)
    step = up * STEPS[2]
    p = step * amplitudes[7]
    d = p
    p = amplitudes[6] + p
    for m in (1, 0):
        step = up * STEPS[m]
        p = step * p
        d = step * d + p
        p = amplitudes[MIDDLE + m] + p
    step = down * STEPS[3]
    s = step * amplitudes[0]
    e = s
    s = amplitudes[1] + s
    for m in (2, 1):
        step = down * STEPS[m]
        s = step * s
        e = step * e + s
        s = amplitudes[MIDDLE - m] + s
    step = down * STEPS[0]
    s = step * s
    e = step * e + s
    p = p + s
    d = d - e
    hc = h * c
    inner = (hc * (-2.0 * GAMMA) - 2.0 / CUTOFF_SQUARED) * p + (c * (2.0 * GAMMA * CENTER_STEP)) * d
    return (middle * c) * inner


def pairs(shift_ref, own_ref, weights_ref, column_ref, before_ref, forces_ref):
    own = own_ref[2 * BOX :, :BOX].astype(jnp.float32) * PITCH
    theirs = column_ref[4 * BOX :, :BOX].astype(jnp.float32) * PITCH
    theirs = jnp.transpose(jnp.concatenate([theirs, jnp.zeros((BOX - 16, BOX), jnp.float32)], axis=0))
    across = shift_ref[0] * PITCH
    results = [[None, None] for _ in range(3)]
    for b in range(2):
        mine = [own[2 * c + b : 2 * c + b + 1] for c in range(3)]
        totals = [jnp.zeros((ROWS, BOX), jnp.float32) for _ in range(3)]
        for upward in range(3):
            s = b + upward
            product = lax.dot_general(
                column_ref[s * BOX : (s + 1) * BOX, :],
                weights_ref[b],
                (((1,), (1,)), ((), ())),
                preferred_element_type=jnp.float32,
            )
            shifts = [across, (upward - 1) * PITCH, 0.0]
            for r in range(0, BOX, ROWS):
                along = [
                    (theirs[r : r + ROWS, 4 * c + s : 4 * c + s + 1] + shifts[c]) - mine[c] for c in range(3)
                ]
                strength = strengths(
                    *along, [product[r : r + ROWS, k * BOX : (k + 1) * BOX] for k in range(RADIAL)]
                )
                totals = [t + strength * a for t, a in zip(totals, along, strict=True)]
        for c in range(3):
            results[c][b] = jnp.sum(totals[c], axis=0, keepdims=True) * (2.0 * FORCE_UNIT)
    for c in range(3):
        forces_ref[c] = before_ref[c] + jnp.concatenate(results[c], axis=0)


def swap(x, axis, later):
    n = lax.axis_size(axis)
    if later:
        perm = [(i, (i + 1) % n if i % 2 else (i - 1) % n) for i in range(n)]
    else:
        perm = [(i, i + 1 - 2 * (i % 2)) for i in range(n)]
    return lax.ppermute(x, axis, perm)


def on_device(offsets, features, cotangent, w_in, w_out, w_filter, counts):
    bf16 = jnp.bfloat16
    odd = (lax.axis_index("tower") % 2).astype(jnp.int32)[None]
    side = 1.0 - 2.0 * (lax.axis_index("plane") % 2).astype(jnp.float32)[None]
    turned = jnp.transpose(offsets[0], (1, 0, 2))
    own, first, second = pl.pallas_call(
        prepare,
        out_shape=(
            jax.ShapeDtypeStruct((2 * BOX + 16, 2 * F), bf16),
            jax.ShapeDtypeStruct((BOX + 16, 2 * F), bf16),
            jax.ShapeDtypeStruct((BOX + 16, 2 * F), bf16),
        ),
        in_specs=[smem(), smem()] + [vmem()] * 5,
        out_specs=(vmem(),) * 3,
        compiler_params=params(16),
        name="prepare",
    )(odd, counts, turned, features[0], cotangent[0], w_in, w_out)
    second = swap(second, "tower", True)
    first = swap(first, "tower", False)
    weights = pl.pallas_call(
        spread_weights,
        out_shape=jax.ShapeDtypeStruct((2, RADIAL * BOX, 2 * F), bf16),
        in_specs=[vmem()] * 2,
        out_specs=vmem(),
        compiler_params=params(16),
        name="spread_weights",
    )(own, w_filter)
    column = pl.pallas_call(
        join,
        out_shape=jax.ShapeDtypeStruct((4 * BOX + 16, 2 * F), bf16),
        in_specs=[smem()] + [vmem()] * 3,
        out_specs=vmem(),
        compiler_params=params(16),
        name="join",
    )(odd, own, first, second)
    outer = swap(column, "plane", True)
    inner = swap(column, "plane", False)
    forces = jnp.zeros((3, 2, BOX), jnp.float32)
    for name, shift, source in (("same", side * 0.0, column), ("inner", side, inner), ("outer", -side, outer)):
        forces = pl.pallas_call(
            pairs,
            out_shape=jax.ShapeDtypeStruct((3, 2, BOX), jnp.float32),
            in_specs=[smem()] + [vmem()] * 4,
            out_specs=vmem(),
            compiler_params=params(32),
            cost_estimate=pl.CostEstimate(flops=6 * 2**27, bytes_accessed=2**21, transcendentals=0),
            name="pairs_" + name,
        )(shift, own, weights, source, forces)
    return jnp.transpose(forces, (1, 0, 2))[None]


def solution(mesh):
    placed = (
        P("plane", "tower", None, None),
        P("plane", "tower", None, None),
        P("plane", "tower", None, None),
        P(),
        P(),
        P(),
        P("plane", "tower"),
    )
    return jax.shard_map(
        on_device,
        mesh=mesh,
        in_specs=placed,
        out_specs=P("plane", "tower", None, None),
        check_vma=False,
    )
```

```python
import math

import jax
import jax.numpy as jnp
from jax import lax
from jax.experimental import pallas as pl
from jax.experimental.pallas import tpu as pltpu
from jax.sharding import PartitionSpec as P

PITCH = 12.5
CUTOFF = 5.0
CENTER_STEP = 3.125
GAMMA = 0.2
FORCE_UNIT = 0.005
LOG2E = math.log2(math.e)

BOX = 128
F = 256
RADIAL = 8
MIDDLE = 4
ROWS = 16

LENGTH = PITCH / CUTOFF
SPREAD = GAMMA * CENTER_STEP**2
FACTORS = [math.exp(-SPREAD * (k - MIDDLE) ** 2) for k in range(RADIAL)]
OFFSET = 2.0 / CUTOFF**2 / (2.0 * GAMMA * CENTER_STEP)
SCALE = -2.0 * GAMMA * CENTER_STEP * CUTOFF * 2.0 * FORCE_UNIT

NN = (((1,), (0,)), ((), ()))
NT = (((1,), (1,)), ((), ()))
BF16 = jnp.bfloat16
F32 = jnp.float32


def vmem():
    return pl.BlockSpec(memory_space=pltpu.VMEM)


def hbm():
    return pl.BlockSpec(memory_space=pltpu.HBM)


def params(mib):
    return pltpu.CompilerParams(vmem_limit_bytes=mib * 2**20)


def shape(*dims, dtype=F32):
    return jax.ShapeDtypeStruct(dims, dtype)


def packed_offsets(rows):
    tall = jnp.concatenate([rows, jnp.zeros((16 - rows.shape[0], BOX), F32)], axis=0)
    wide = jnp.concatenate([tall, jnp.zeros((16, 2 * F - BOX), F32)], axis=1)
    return wide.astype(BF16)


def prepare(
    counts_ref, offsets_ref, features_ref, cotangent_ref, w_in_ref, w_out_ref, w_filter_ref,
    own_ref, first_ref, second_ref, filter_ref,
    counts, offsets_in, features, cotangent, w_in, w_out, sems,
):
    moves = [
        pltpu.make_async_copy(source, target, sems.at[i])
        for i, (source, target) in enumerate(
            [
                (features_ref, features), (w_in_ref, w_in), (cotangent_ref, cotangent), (w_out_ref, w_out),
                (counts_ref, counts), (offsets_ref, offsets_in), (w_filter_ref, filter_ref),
            ]
        )
    ]
    for move in moves:
        move.start()
    for move in moves:
        move.wait()
    odd = lax.rem(lax.axis_index("tower"), 2) == 1
    slots = lax.broadcasted_iota(jnp.int32, (BOX, F), 0)
    offsets = offsets_in[...].astype(F32)
    boxes = []
    for b in range(2):
        live = slots < counts[0, b]
        values = jnp.dot(features[b], w_in[...], preferred_element_type=F32)
        grads = lax.dot_general(cotangent[b], w_out[...], NT, preferred_element_type=F32)
        both = jnp.concatenate([jnp.where(live, values, 0.0), jnp.where(live, grads, 0.0)], axis=1)
        boxes.append(both)
        own_ref[b * BOX : (b + 1) * BOX, :] = both.astype(BF16)
    own_ref[2 * BOX :, :] = packed_offsets(offsets.reshape(6, BOX))
    first_ref[:BOX, :] = jnp.where(odd, boxes[0], boxes[1]).astype(BF16)
    second_ref[:BOX, :] = jnp.where(odd, boxes[1], boxes[0]).astype(BF16)
    first_ref[BOX:, :] = packed_offsets(jnp.where(odd, offsets[:, 0], offsets[:, 1]))
    second_ref[BOX:, :] = packed_offsets(jnp.where(odd, offsets[:, 1], offsets[:, 0]))


def join(second_ref, first_ref, outer_ref):
    odd = lax.rem(lax.axis_index("tower"), 2) == 1
    first = first_ref[...].astype(F32)
    second = second_ref[...].astype(F32)
    below = jnp.where(odd, first, second)
    above = jnp.where(odd, second, first)
    outer_ref[:BOX, :] = below[:BOX].astype(BF16)
    outer_ref[BOX : 2 * BOX, :] = above[:BOX].astype(BF16)
    rows = []
    for c in range(3):
        rows += [below[BOX + c : BOX + c + 1, :BOX], above[BOX + c : BOX + c + 1, :BOX]]
    outer_ref[2 * BOX :, :] = packed_offsets(jnp.concatenate(rows, axis=0))


def strengths(dx, dy, dz, a):
    c = jnp.maximum(1.0 - (dx * dx + dy * dy + dz * dz), 0.0)
    h = MIDDLE - RADIAL * c
    middle = jnp.exp2(h * h * (-SPREAD * LOG2E))
    up = jnp.exp2(h * (2.0 * SPREAD * LOG2E))
    down = jnp.exp2(h * (-2.0 * SPREAD * LOG2E))
    s = up * a[7]
    d = s
    p = a[6] + s
    for k in (5, 4):
        s = up * p
        d = up * d + s
        p = a[k] + s
    s = down * a[0]
    e = s
    for k in (1, 2, 3):
        s = down * (a[k] + s)
        e = down * e + s
    p = p + s
    d = d - e
    return (middle * c) * ((h * c + OFFSET) * p - c * d)


def rows_of(ref):
    return ref[2 * BOX :, :BOX].astype(F32) * LENGTH


def columns_of(ref):
    rows = rows_of(ref)
    return jnp.transpose(jnp.concatenate([rows, jnp.zeros((BOX - 16, BOX), F32)], axis=0))


def box_of(ref, b):
    return ref[b * BOX : (b + 1) * BOX, :]


def targets(rows, b, shifts):
    return [rows[2 * c + b : 2 * c + b + 1] - shifts[c] * LENGTH for c in range(3)]


def sources(columns, b, r):
    return [jnp.broadcast_to(columns[r : r + ROWS, 2 * c + b : 2 * c + b + 1], (ROWS, BOX)) for c in range(3)]


def zeros():
    return [jnp.zeros((ROWS, BOX), F32) for _ in range(3)]


def tile(product, r):
    return [product[r : r + ROWS, k * BOX : (k + 1) * BOX] for k in range(RADIAL)]


def total(t):
    return jnp.sum(t, axis=0, keepdims=True) * SCALE


def spread(own_ref, w_filter_ref, weights_ref):
    w = jnp.transpose(
        jnp.concatenate([w_filter_ref[...].astype(F32), jnp.zeros((BOX - RADIAL, F), F32)], axis=0)
    )
    for b in range(2):
        both = jnp.transpose(box_of(own_ref, b).astype(F32))
        for k in range(RADIAL):
            column = jnp.broadcast_to(w[:, k : k + 1] * FACTORS[k], (F, BOX))
            weights_ref[b, :F, k * BOX : (k + 1) * BOX] = (both[F:] * column).astype(BF16)
            weights_ref[b, F:, k * BOX : (k + 1) * BOX] = (both[:F] * column).astype(BF16)


def within(own_ref, w_filter_ref, weights_ref, forces_ref):
    spread(own_ref, w_filter_ref, weights_ref)
    rows, columns = rows_of(own_ref), columns_of(own_ref)
    sums = [zeros(), zeros()]
    for s in range(2):
        products = [
            lax.dot_general(box_of(own_ref, s), weights_ref[b], NN, preferred_element_type=F32) for b in range(2)
        ]
        mine = [targets(rows, b, (0.0, float(s - b), 0.0)) for b in range(2)]
        for r in range(0, BOX, ROWS):
            theirs = sources(columns, s, r)
            for b in range(2):
                along = [t - m for t, m in zip(theirs, mine[b], strict=True)]
                strength = strengths(*along, tile(products[b], r))
                sums[b] = [t + strength * a for t, a in zip(sums[b], along, strict=True)]
    for c in range(3):
        forces_ref[c] = jnp.concatenate([total(sums[0][c]), total(sums[1][c])], axis=0)


def across(own_ref, outer_ref, before_ref, w_filter_ref, weights_ref, so_far_ref, forces_ref, back_ref, filtered, turned):
    lane = lax.broadcasted_iota(jnp.int32, (ROWS, BOX), 1)
    own, outer, columns = rows_of(own_ref), rows_of(outer_ref), columns_of(before_ref)
    sums = [zeros(), zeros()]
    for s in range(2):
        source = box_of(before_ref, s)
        products = [lax.dot_general(source, weights_ref[b], NN, preferred_element_type=F32) for b in range(2)]
        wide = source.astype(F32)
        for k in range(RADIAL):
            w = w_filter_ref[k : k + 1, :].astype(F32) * FACTORS[k]
            filtered[s, k * BOX : (k + 1) * BOX, :F] = (wide[:, F:] * w).astype(BF16)
            filtered[s, k * BOX : (k + 1) * BOX, F:] = (wide[:, :F] * w).astype(BF16)
        corner = lax.dot_general(filtered[s], box_of(outer_ref, s), NT, preferred_element_type=F32)
        mine = [targets(own, b, (-1.0, float(s - b), 0.0)) for b in range(2)]
        diagonal = targets(outer, s, (-1.0, 1.0 - 2.0 * s, 0.0))
        for r in range(0, BOX, ROWS):
            theirs = sources(columns, s, r)
            along = [t - m for t, m in zip(theirs, diagonal, strict=True)]
            strength = strengths(*along, [corner[k * BOX + r : k * BOX + r + ROWS] for k in range(RADIAL)])
            back = [strength * a for a in along]
            for b in range(2):
                along = [t - m for t, m in zip(theirs, mine[b], strict=True)]
                strength = strengths(*along, tile(products[b], r))
                terms = [strength * a for a in along]
                sums[b] = [t + u for t, u in zip(sums[b], terms, strict=True)]
                back = [t + u for t, u in zip(back, terms, strict=True)]
            x, y, z = [jnp.sum(t, axis=1, keepdims=True) * -SCALE for t in back]
            turned[s, r : r + ROWS, :] = jnp.where(lane == 0, x, jnp.where(lane == 1, y, z))
    for c in range(3):
        forces_ref[c] = so_far_ref[c] + jnp.concatenate([total(sums[0][c]), total(sums[1][c])], axis=0)
    backs = [jnp.transpose(turned[s]) for s in range(2)]
    for c in range(3):
        back_ref[c] = jnp.concatenate([backs[s][c : c + 1] for s in range(2)], axis=0)


def outer_pairs(own_ref, outer_ref, weights_ref, shift):
    rows, columns = rows_of(own_ref), columns_of(outer_ref)
    sums = []
    for s in range(2):
        product = lax.dot_general(box_of(outer_ref, s), weights_ref[s], NN, preferred_element_type=F32)
        mine = targets(rows, s, (shift, 2.0 * s - 1.0, 0.0))
        t = zeros()
        for r in range(0, BOX, ROWS):
            along = [u - m for u, m in zip(sources(columns, s, r), mine, strict=True)]
            strength = strengths(*along, tile(product, r))
            t = [u + strength * a for u, a in zip(t, along, strict=True)]
        sums.append(t)
    return [jnp.concatenate([total(sums[0][c]), total(sums[1][c])], axis=0) for c in range(3)]


def beside(own_ref, outer_ref, weights_ref, so_far_ref, forces_ref):
    added = outer_pairs(own_ref, outer_ref, weights_ref, 0.0)
    for c in range(3):
        forces_ref[c] = so_far_ref[c] + added[c]


def finish(own_ref, outer_ref, weights_ref, so_far_ref, returned_ref, forces_ref):
    added = outer_pairs(own_ref, outer_ref, weights_ref, -1.0)
    for c in range(3):
        forces_ref[c] = (so_far_ref[c] + returned_ref[c]) + added[c]


def swap(x, axis, later):
    n = lax.axis_size(axis)
    if later:
        perm = [(i, (i + 1) % n if i % 2 else (i - 1) % n) for i in range(n)]
    else:
        perm = [(i, i + 1 - 2 * (i % 2)) for i in range(n)]
    return lax.ppermute(x, axis, perm)


def pass_on(x, axis, step):
    n = lax.axis_size(axis)
    return lax.ppermute(x, axis, [(i, (i + step) % n) for i in range(n)])


def kernel(body, name, out_shape, n_in, pair_count=0, scratch_shapes=()):
    return pl.pallas_call(
        body,
        out_shape=out_shape,
        in_specs=[vmem()] * n_in,
        out_specs=jax.tree.map(lambda _: vmem(), out_shape),
        scratch_shapes=list(scratch_shapes),
        compiler_params=params(40),
        cost_estimate=pl.CostEstimate(flops=pair_count * 2**27, bytes_accessed=2**18, transcendentals=0),
        name=name,
    )


def on_device(offsets, features, cotangent, w_in, w_out, w_filter, counts):
    turned = jnp.transpose(offsets[0], (1, 0, 2))
    forces_shape = shape(3, 2, BOX)
    own, first, second, filters = pl.pallas_call(
        prepare,
        out_shape=(
            shape(2 * BOX + 16, 2 * F, dtype=BF16),
            shape(BOX + 16, 2 * F, dtype=BF16),
            shape(BOX + 16, 2 * F, dtype=BF16),
            shape(RADIAL, F, dtype=BF16),
        ),
        in_specs=[hbm()] * 7,
        out_specs=(vmem(),) * 4,
        scratch_shapes=[
            pltpu.SMEM((1, 2), jnp.int32),
            pltpu.VMEM((3, 2, BOX), BF16),
            pltpu.VMEM((2, BOX, F), BF16),
            pltpu.VMEM((2, BOX, F), BF16),
            pltpu.VMEM((F, F), BF16),
            pltpu.VMEM((F, F), BF16),
            pltpu.SemaphoreType.DMA((7,)),
        ],
        compiler_params=params(16),
        name="prepare",
    )(*[pltpu.with_memory_space_constraint(x, pltpu.HBM) for x in (counts, turned, features[0], cotangent[0], w_in, w_out, w_filter)])
    second = swap(second, "tower", True)
    before = pass_on(own, "plane", 1)
    first = swap(first, "tower", False)
    weights, forces = kernel(
        within, "within", (shape(2, 2 * F, RADIAL * BOX, dtype=BF16), forces_shape), 2, 4
    )(own, filters)
    outer = kernel(join, "join", shape(2 * BOX + 16, 2 * F, dtype=BF16), 2)(second, first)
    before_outer = pass_on(outer, "plane", 1)
    forces, back = kernel(
        across,
        "across",
        (forces_shape, forces_shape),
        6,
        8,
        [pltpu.VMEM((2, RADIAL * BOX, 2 * F), BF16), pltpu.VMEM((2, BOX, BOX), F32)],
    )(own, outer, before, filters, weights, forces)
    returned = pass_on(back, "plane", -1)
    forces = kernel(beside, "beside", forces_shape, 4, 2)(own, outer, weights, forces)
    forces = kernel(finish, "finish", forces_shape, 5, 2)(own, before_outer, weights, forces, returned)
    return jnp.transpose(forces, (1, 0, 2))[None]


def solution(mesh):
    placed = (
        P("plane", "tower", None, None),
        P("plane", "tower", None, None),
        P("plane", "tower", None, None),
        P(),
        P(),
        P(),
        P("plane", "tower"),
    )
    return jax.shard_map(
        on_device,
        mesh=mesh,
        in_specs=placed,
        out_specs=P("plane", "tower", None, None),
        check_vma=False,
    )
```

```python
import math

import jax
import jax.numpy as jnp
from jax import lax
from jax.experimental import pallas as pl
from jax.experimental.pallas import tpu as pltpu
from jax.sharding import PartitionSpec as P

PITCH = 12.5
CUTOFF = 5.0
CENTER_STEP = 3.125
GAMMA = 0.2
FORCE_UNIT = 0.005
LOG2E = math.log2(math.e)

BOX = 128
F = 256
RADIAL = 8
MIDDLE = 4
ROWS = 32
TAIL = 8

LENGTH = PITCH / CUTOFF
SPREAD = GAMMA * CENTER_STEP**2
FACTORS = [math.exp(-SPREAD * (k - MIDDLE) ** 2) for k in range(RADIAL)]
OFFSET = 2.0 / CUTOFF**2 / (2.0 * GAMMA * CENTER_STEP)
SCALE = -2.0 * GAMMA * CENTER_STEP * CUTOFF * 2.0 * FORCE_UNIT

NN = (((1,), (0,)), ((), ()))
NT = (((1,), (1,)), ((), ()))
BF16 = jnp.bfloat16
F32 = jnp.float32


def vmem():
    return pl.BlockSpec(memory_space=pltpu.VMEM)


def hbm():
    return pl.BlockSpec(memory_space=pltpu.HBM)


def params(mib):
    return pltpu.CompilerParams(vmem_limit_bytes=mib * 2**20)


def shape(*dims, dtype=F32):
    return jax.ShapeDtypeStruct(dims, dtype)


def packed_offsets(rows):
    tall = jnp.concatenate([rows, jnp.zeros((TAIL - rows.shape[0], BOX), F32)], axis=0)
    wide = jnp.concatenate([tall, jnp.zeros((TAIL, 2 * F - BOX), F32)], axis=1)
    return wide.astype(BF16)


def prepare(
    counts_ref, offsets_ref, features_ref, cotangent_ref, w_in_ref, w_out_ref, w_filter_ref,
    own_ref, first_ref, second_ref, filter_ref,
    counts, offsets_in, features, cotangent, w_in, w_out, sems,
):
    moves = [
        pltpu.make_async_copy(source, target, sems.at[i])
        for i, (source, target) in enumerate(
            [
                (features_ref, features), (w_in_ref, w_in), (cotangent_ref, cotangent), (w_out_ref, w_out),
                (counts_ref, counts), (offsets_ref, offsets_in), (w_filter_ref, filter_ref),
            ]
        )
    ]
    for move in moves:
        move.start()
    odd = lax.rem(lax.axis_index("tower"), 2)
    slots = lax.broadcasted_iota(jnp.int32, (BOX, F), 0)
    for i in (0, 1, 4):
        moves[i].wait()
    for b in range(2):
        values = jnp.dot(features[b], w_in[...], preferred_element_type=F32)
        own_ref[b * BOX : (b + 1) * BOX, :F] = jnp.where(slots < counts[0, b], values, 0.0).astype(BF16)
    for i in (2, 3, 5, 6):
        moves[i].wait()
    for b in range(2):
        grads = lax.dot_general(cotangent[b], w_out[...], NT, preferred_element_type=F32)
        own_ref[b * BOX : (b + 1) * BOX, F:] = jnp.where(slots < counts[0, b], grads, 0.0).astype(BF16)
    offsets = offsets_in[...].astype(F32)
    own_ref[2 * BOX :, :] = packed_offsets(offsets.reshape(6, BOX))
    first_ref[:BOX, :] = own_ref[pl.ds(pl.multiple_of((1 - odd) * BOX, BOX), BOX), :]
    second_ref[:BOX, :] = own_ref[pl.ds(pl.multiple_of(odd * BOX, BOX), BOX), :]
    first_ref[BOX:, :] = packed_offsets(jnp.where(odd == 1, offsets[:, 0], offsets[:, 1]))
    second_ref[BOX:, :] = packed_offsets(jnp.where(odd == 1, offsets[:, 1], offsets[:, 0]))


def join(second_ref, first_ref, weights_ref, outer_ref):
    odd = lax.rem(lax.axis_index("tower"), 2) == 1
    first = first_ref[...].astype(F32)
    second = second_ref[...].astype(F32)
    below = jnp.where(odd, first, second)
    above = jnp.where(odd, second, first)
    outer_ref[:BOX, :] = below[:BOX].astype(BF16)
    outer_ref[BOX : 2 * BOX, :] = above[:BOX].astype(BF16)
    rows = []
    for c in range(3):
        rows += [below[BOX + c : BOX + c + 1, :BOX], above[BOX + c : BOX + c + 1, :BOX]]
    outer_ref[2 * BOX :, :] = packed_offsets(jnp.concatenate(rows, axis=0))


def strengths(dx, dy, dz, a):
    c = jnp.maximum(1.0 - (dx * dx + dy * dy + dz * dz), 0.0)
    h = MIDDLE - RADIAL * c
    middle = jnp.exp2(h * h * (-SPREAD * LOG2E))
    up = jnp.exp2(h * (2.0 * SPREAD * LOG2E))
    down = jnp.exp2(h * (-2.0 * SPREAD * LOG2E))
    s = up * a[7]
    d = s
    p = a[6] + s
    for k in (5, 4):
        s = up * p
        d = up * d + s
        p = a[k] + s
    s = down * a[0]
    e = s
    for k in (1, 2, 3):
        s = down * (a[k] + s)
        e = down * e + s
    p = p + s
    d = d - e
    return (middle * c) * ((h * c + OFFSET) * p - c * d)


def rows_of(ref):
    return ref[2 * BOX :, :BOX].astype(F32) * LENGTH


def columns_of(ref):
    rows = rows_of(ref)
    return jnp.transpose(jnp.concatenate([rows, jnp.zeros((BOX - TAIL, BOX), F32)], axis=0))


def box_of(ref, b):
    return ref[b * BOX : (b + 1) * BOX, :]


def targets(rows, b, shifts):
    return [rows[2 * c + b : 2 * c + b + 1] - shifts[c] * LENGTH for c in range(3)]


def sources(columns, b, r):
    return [jnp.broadcast_to(columns[r : r + ROWS, 2 * c + b : 2 * c + b + 1], (ROWS, BOX)) for c in range(3)]


def zeros():
    return [jnp.zeros((ROWS, BOX), F32) for _ in range(3)]


def tile(product, r):
    return [product[r : r + ROWS, k * BOX : (k + 1) * BOX] for k in range(RADIAL)]


def total(t):
    return jnp.sum(t, axis=0, keepdims=True) * SCALE


def spread(own_ref, w_filter_ref, weights_ref):
    w = jnp.transpose(
        jnp.concatenate([w_filter_ref[...].astype(F32), jnp.zeros((BOX - RADIAL, F), F32)], axis=0)
    )
    turned = [jnp.transpose(box_of(own_ref, b).astype(F32)) for b in range(2)]
    for k in range(RADIAL):
        broad = jnp.broadcast_to(w[:, k : k + 1] * FACTORS[k], (F, BOX))
        for b, both in enumerate(turned):
            weights_ref[b, :F, k * BOX : (k + 1) * BOX] = (both[F:] * broad).astype(BF16)
            weights_ref[b, F:, k * BOX : (k + 1) * BOX] = (both[:F] * broad).astype(BF16)


def within(own_ref, weights_ref):
    rows, columns = rows_of(own_ref), columns_of(own_ref)
    sums = [zeros(), zeros()]
    for s in range(2):
        products = [
            lax.dot_general(box_of(own_ref, s), weights_ref[b], NN, preferred_element_type=F32) for b in range(2)
        ]
        mine = [targets(rows, b, (0.0, float(s - b), 0.0)) for b in range(2)]
        for r in range(0, BOX, ROWS):
            theirs = sources(columns, s, r)
            for b in range(2):
                along = [t - m for t, m in zip(theirs, mine[b], strict=True)]
                strength = strengths(*along, tile(products[b], r))
                sums[b] = [t + strength * a for t, a in zip(sums[b], along, strict=True)]
    return [jnp.concatenate([total(sums[0][c]), total(sums[1][c])], axis=0) for c in range(3)]


def across(own_ref, outer_ref, before_ref, w_filter_ref, so_far_ref, forces_ref, back_ref, filtered, turned):
    lane = lax.broadcasted_iota(jnp.int32, (ROWS, BOX), 1)
    own, outer, columns = rows_of(own_ref), rows_of(outer_ref), columns_of(before_ref)
    sums = [zeros(), zeros()]
    for s in range(2):
        wide = box_of(before_ref, s).astype(F32)
        for k in range(RADIAL):
            w = w_filter_ref[k : k + 1, :].astype(F32) * FACTORS[k]
            filtered[s, k * BOX : (k + 1) * BOX, :F] = (wide[:, F:] * w).astype(BF16)
            filtered[s, k * BOX : (k + 1) * BOX, F:] = (wide[:, :F] * w).astype(BF16)
        inner = lax.dot_general(filtered[s], own_ref[: 2 * BOX, :], NT, preferred_element_type=F32)
        corner = lax.dot_general(filtered[s], box_of(outer_ref, s), NT, preferred_element_type=F32)
        mine = [targets(own, b, (-1.0, float(s - b), 0.0)) for b in range(2)]
        diagonal = targets(outer, s, (-1.0, 1.0 - 2.0 * s, 0.0))
        for r in range(0, BOX, ROWS):
            theirs = sources(columns, s, r)
            along = [t - m for t, m in zip(theirs, diagonal, strict=True)]
            strength = strengths(*along, [corner[k * BOX + r : k * BOX + r + ROWS] for k in range(RADIAL)])
            back = [strength * a for a in along]
            for b in range(2):
                along = [t - m for t, m in zip(theirs, mine[b], strict=True)]
                strength = strengths(
                    *along,
                    [inner[k * BOX + r : k * BOX + r + ROWS, b * BOX : (b + 1) * BOX] for k in range(RADIAL)],
                )
                terms = [strength * a for a in along]
                sums[b] = [t + u for t, u in zip(sums[b], terms, strict=True)]
                back = [t + u for t, u in zip(back, terms, strict=True)]
            x, y, z = [jnp.sum(t, axis=1, keepdims=True) * -SCALE for t in back]
            turned[s, r : r + ROWS, :] = jnp.where(lane == 0, x, jnp.where(lane == 1, y, z))
    for c in range(3):
        forces_ref[c] = so_far_ref[c] + jnp.concatenate([total(sums[0][c]), total(sums[1][c])], axis=0)
    backs = [jnp.transpose(turned[s]) for s in range(2)]
    for c in range(3):
        back_ref[c] = jnp.concatenate([backs[s][c : c + 1] for s in range(2)], axis=0)


def outer_pairs(own_ref, outer_ref, weights_ref, shift):
    rows, columns = rows_of(own_ref), columns_of(outer_ref)
    sums = []
    for s in range(2):
        product = lax.dot_general(box_of(outer_ref, s), weights_ref[s], NN, preferred_element_type=F32)
        mine = targets(rows, s, (shift, 2.0 * s - 1.0, 0.0))
        t = zeros()
        for r in range(0, BOX, ROWS):
            along = [u - m for u, m in zip(sources(columns, s, r), mine, strict=True)]
            strength = strengths(*along, tile(product, r))
            t = [u + strength * a for u, a in zip(t, along, strict=True)]
        sums.append(t)
    return [jnp.concatenate([total(sums[0][c]), total(sums[1][c])], axis=0) for c in range(3)]


def column(own_ref, outer_ref, weights_ref, forces_ref):
    near, far = within(own_ref, weights_ref), outer_pairs(own_ref, outer_ref, weights_ref, 0.0)
    for c in range(3):
        forces_ref[c] = near[c] + far[c]


def corner(own_ref, outer_ref, weights_ref, so_far_ref, forces_ref):
    added = outer_pairs(own_ref, outer_ref, weights_ref, -1.0)
    for c in range(3):
        forces_ref[c] = so_far_ref[c] + added[c]


def finish(so_far_ref, returned_ref, forces_ref):
    forces_ref[...] = so_far_ref[...] + returned_ref[...]


def swap(x, axis, later):
    n = lax.axis_size(axis)
    if later:
        perm = [(i, (i + 1) % n if i % 2 else (i - 1) % n) for i in range(n)]
    else:
        perm = [(i, i + 1 - 2 * (i % 2)) for i in range(n)]
    return lax.ppermute(x, axis, perm)


def pass_on(x, axis, step):
    n = lax.axis_size(axis)
    return lax.ppermute(x, axis, [(i, (i + step) % n) for i in range(n)])


def kernel(body, name, out_shape, n_in, pair_count=0, scratch_shapes=()):
    return pl.pallas_call(
        body,
        out_shape=out_shape,
        in_specs=[vmem()] * n_in,
        out_specs=jax.tree.map(lambda _: vmem(), out_shape),
        scratch_shapes=list(scratch_shapes),
        compiler_params=params(40),
        cost_estimate=pl.CostEstimate(flops=pair_count * 2**27, bytes_accessed=2**18, transcendentals=0),
        name=name,
    )


def on_device(offsets, features, cotangent, w_in, w_out, w_filter, counts):
    turned = jnp.transpose(offsets[0], (1, 0, 2))
    forces_shape = shape(3, 2, BOX)
    own, first, second, filters = pl.pallas_call(
        prepare,
        out_shape=(
            shape(2 * BOX + TAIL, 2 * F, dtype=BF16),
            shape(BOX + TAIL, 2 * F, dtype=BF16),
            shape(BOX + TAIL, 2 * F, dtype=BF16),
            shape(RADIAL, F, dtype=BF16),
        ),
        in_specs=[hbm()] * 7,
        out_specs=(vmem(),) * 4,
        scratch_shapes=[
            pltpu.SMEM((1, 2), jnp.int32),
            pltpu.VMEM((3, 2, BOX), BF16),
            pltpu.VMEM((2, BOX, F), BF16),
            pltpu.VMEM((2, BOX, F), BF16),
            pltpu.VMEM((F, F), BF16),
            pltpu.VMEM((F, F), BF16),
            pltpu.SemaphoreType.DMA((7,)),
        ],
        compiler_params=params(16),
        name="prepare",
    )(*[pltpu.with_memory_space_constraint(x, pltpu.HBM) for x in (counts, turned, features[0], cotangent[0], w_in, w_out, w_filter)])
    second = swap(second, "tower", True)
    before = pass_on(own, "plane", 1)
    first = swap(first, "tower", False)
    weights = kernel(spread, "spread", shape(2, 2 * F, RADIAL * BOX, dtype=BF16), 2, 0)(own, filters)
    outer = kernel(join, "join", shape(2 * BOX + TAIL, 2 * F, dtype=BF16), 3)(second, first, weights)
    before_outer = pass_on(outer, "plane", 1)
    forces = kernel(column, "column", forces_shape, 3, 2)(own, outer, weights)
    forces, back = kernel(
        across,
        "across",
        (forces_shape, forces_shape),
        5,
        8,
        [pltpu.VMEM((2, RADIAL * BOX, 2 * F), BF16), pltpu.VMEM((2, BOX, BOX), F32)],
    )(own, outer, before, filters, forces)
    returned = pass_on(back, "plane", -1)
    forces = kernel(corner, "corner", forces_shape, 4, 2)(own, before_outer, weights, forces)
    forces = kernel(finish, "finish", forces_shape, 2)(forces, returned)
    return jnp.transpose(forces, (1, 0, 2))[None]


def solution(mesh):
    placed = (
        P("plane", "tower", None, None),
        P("plane", "tower", None, None),
        P("plane", "tower", None, None),
        P(),
        P(),
        P(),
        P("plane", "tower"),
    )
    return jax.shard_map(
        on_device,
        mesh=mesh,
        in_specs=placed,
        out_specs=P("plane", "tower", None, None),
        check_vma=False,
    )
```

```python
import math

import jax
import jax.numpy as jnp
from jax import lax
from jax.experimental import pallas as pl
from jax.experimental.pallas import tpu as pltpu
from jax.sharding import PartitionSpec as P

PITCH = 12.5
CUTOFF = 5.0
CENTER_STEP = 3.125
GAMMA = 0.2
FORCE_UNIT = 0.005
LOG2E = math.log2(math.e)

BOX = 128
F = 256
RADIAL = 8
MIDDLE = 4
ROWS = 32
TAIL = 8

LENGTH = PITCH / CUTOFF
SPREAD = GAMMA * CENTER_STEP**2
FACTORS = [math.exp(-SPREAD * (k - MIDDLE) ** 2) for k in range(RADIAL)]
OFFSET = 2.0 / CUTOFF**2 / (2.0 * GAMMA * CENTER_STEP)
SCALE = -2.0 * GAMMA * CENTER_STEP * CUTOFF * 2.0 * FORCE_UNIT

NN = (((1,), (0,)), ((), ()))
NT = (((1,), (1,)), ((), ()))
BF16 = jnp.bfloat16
F32 = jnp.float32


def vmem():
    return pl.BlockSpec(memory_space=pltpu.VMEM)


def hbm():
    return pl.BlockSpec(memory_space=pltpu.HBM)


def params(mib):
    return pltpu.CompilerParams(vmem_limit_bytes=mib * 2**20)


def shape(*dims, dtype=F32):
    return jax.ShapeDtypeStruct(dims, dtype)


def packed_offsets(rows):
    tall = jnp.concatenate([rows, jnp.zeros((TAIL - rows.shape[0], BOX), F32)], axis=0)
    wide = jnp.concatenate([tall, jnp.zeros((TAIL, 2 * F - BOX), F32)], axis=1)
    return wide.astype(BF16)


def prepare(
    counts_ref, offsets_ref, features_ref, cotangent_ref, w_in_ref, w_out_ref, w_filter_ref,
    own_ref, first_ref, second_ref, filter_ref,
    counts, offsets_in, features, cotangent, w_in, w_out, sems,
):
    moves = [
        pltpu.make_async_copy(source, target, sems.at[i])
        for i, (source, target) in enumerate(
            [
                (features_ref, features), (w_in_ref, w_in), (cotangent_ref, cotangent), (w_out_ref, w_out),
                (counts_ref, counts), (offsets_ref, offsets_in), (w_filter_ref, filter_ref),
            ]
        )
    ]
    for move in moves:
        move.start()
    odd = lax.rem(lax.axis_index("tower"), 2)
    slots = lax.broadcasted_iota(jnp.int32, (BOX, F), 0)
    for i in (0, 1, 4):
        moves[i].wait()
    for b in range(2):
        values = jnp.dot(features[b], w_in[...], preferred_element_type=F32)
        own_ref[b * BOX : (b + 1) * BOX, :F] = jnp.where(slots < counts[0, b], values, 0.0).astype(BF16)
    for i in (2, 3, 5, 6):
        moves[i].wait()
    for b in range(2):
        grads = lax.dot_general(cotangent[b], w_out[...], NT, preferred_element_type=F32)
        own_ref[b * BOX : (b + 1) * BOX, F:] = jnp.where(slots < counts[0, b], grads, 0.0).astype(BF16)
    offsets = offsets_in[...].astype(F32)
    own_ref[2 * BOX :, :] = packed_offsets(offsets.reshape(6, BOX))
    first_ref[:BOX, :] = own_ref[pl.ds(pl.multiple_of((1 - odd) * BOX, BOX), BOX), :]
    second_ref[:BOX, :] = own_ref[pl.ds(pl.multiple_of(odd * BOX, BOX), BOX), :]
    first_ref[BOX:, :] = packed_offsets(jnp.where(odd == 1, offsets[:, 0], offsets[:, 1]))
    second_ref[BOX:, :] = packed_offsets(jnp.where(odd == 1, offsets[:, 1], offsets[:, 0]))


def join(second_ref, first_ref, weights_ref, outer_ref):
    odd = lax.rem(lax.axis_index("tower"), 2) == 1
    first = first_ref[...].astype(F32)
    second = second_ref[...].astype(F32)
    below = jnp.where(odd, first, second)
    above = jnp.where(odd, second, first)
    outer_ref[:BOX, :] = below[:BOX].astype(BF16)
    outer_ref[BOX : 2 * BOX, :] = above[:BOX].astype(BF16)
    rows = []
    for c in range(3):
        rows += [below[BOX + c : BOX + c + 1, :BOX], above[BOX + c : BOX + c + 1, :BOX]]
    outer_ref[2 * BOX :, :] = packed_offsets(jnp.concatenate(rows, axis=0))


def strengths(dx, dy, dz, a):
    c = jnp.maximum(1.0 - (dx * dx + dy * dy + dz * dz), 0.0)
    h = MIDDLE - RADIAL * c
    middle = jnp.exp2(h * h * (-SPREAD * LOG2E))
    up = jnp.exp2(h * (2.0 * SPREAD * LOG2E))
    down = jnp.exp2(h * (-2.0 * SPREAD * LOG2E))
    s = up * a[7]
    d = s
    p = a[6] + s
    for k in (5, 4):
        s = up * p
        d = up * d + s
        p = a[k] + s
    s = down * a[0]
    e = s
    for k in (1, 2, 3):
        s = down * (a[k] + s)
        e = down * e + s
    p = p + s
    d = d - e
    return (middle * c) * ((h * c + OFFSET) * p - c * d)


def rows_of(ref):
    return ref[2 * BOX :, :BOX].astype(F32) * LENGTH


def columns_of(ref):
    rows = rows_of(ref)
    return jnp.transpose(jnp.concatenate([rows, jnp.zeros((BOX - TAIL, BOX), F32)], axis=0))


def box_of(ref, b):
    return ref[b * BOX : (b + 1) * BOX, :]


def targets(rows, b, shifts):
    return [rows[2 * c + b : 2 * c + b + 1] - shifts[c] * LENGTH for c in range(3)]


def sources(columns, b, r):
    return [jnp.broadcast_to(columns[r : r + ROWS, 2 * c + b : 2 * c + b + 1], (ROWS, BOX)) for c in range(3)]


def zeros():
    return [jnp.zeros((ROWS, BOX), F32) for _ in range(3)]


def tile(product, r):
    return [product[r : r + ROWS, k * BOX : (k + 1) * BOX] for k in range(RADIAL)]


def total(t):
    return jnp.sum(t, axis=0, keepdims=True) * SCALE


def spread(own_ref, w_filter_ref, weights_ref):
    lanes = lax.broadcasted_iota(jnp.int32, (RADIAL, RADIAL * BOX), 1) // BOX
    picks = (lanes == lax.broadcasted_iota(jnp.int32, (RADIAL, RADIAL * BOX), 0)).astype(F32).astype(BF16)
    w = lax.dot_general(w_filter_ref[...], picks, (((0,), (0,)), ((), ())), preferred_element_type=F32)
    turned = [jnp.transpose(box_of(own_ref, b).astype(F32)) for b in range(2)]
    for k in range(RADIAL):
        broad = w[:, k * BOX : (k + 1) * BOX] * FACTORS[k]
        for b, both in enumerate(turned):
            weights_ref[b, :F, k * BOX : (k + 1) * BOX] = (both[F:] * broad).astype(BF16)
            weights_ref[b, F:, k * BOX : (k + 1) * BOX] = (both[:F] * broad).astype(BF16)


def within(own_ref, weights_ref):
    rows, columns = rows_of(own_ref), columns_of(own_ref)
    sums = [zeros(), zeros()]
    for s in range(2):
        products = [
            lax.dot_general(box_of(own_ref, s), weights_ref[b], NN, preferred_element_type=F32) for b in range(2)
        ]
        mine = [targets(rows, b, (0.0, float(s - b), 0.0)) for b in range(2)]
        for r in range(0, BOX, ROWS):
            theirs = sources(columns, s, r)
            for b in range(2):
                along = [t - m for t, m in zip(theirs, mine[b], strict=True)]
                strength = strengths(*along, tile(products[b], r))
                sums[b] = [t + strength * a for t, a in zip(sums[b], along, strict=True)]
    return [jnp.concatenate([total(sums[0][c]), total(sums[1][c])], axis=0) for c in range(3)]


def across(own_ref, outer_ref, before_ref, w_filter_ref, so_far_ref, forces_ref, back_ref, filtered, turned):
    lane = lax.broadcasted_iota(jnp.int32, (ROWS, BOX), 1)
    own, outer, columns = rows_of(own_ref), rows_of(outer_ref), columns_of(before_ref)
    sums = [zeros(), zeros()]
    ready = []
    for s in range(2):
        wide = box_of(before_ref, s).astype(F32)
        for k in range(RADIAL):
            w = w_filter_ref[k : k + 1, :].astype(F32) * FACTORS[k]
            filtered[s, k * BOX : (k + 1) * BOX, :F] = (wide[:, F:] * w).astype(BF16)
            filtered[s, k * BOX : (k + 1) * BOX, F:] = (wide[:, :F] * w).astype(BF16)
        inner = lax.dot_general(filtered[s], own_ref[: 2 * BOX, :], NT, preferred_element_type=F32)
        corner = lax.dot_general(filtered[s], box_of(outer_ref, s), NT, preferred_element_type=F32)
        ready.append((inner, corner))
    for s in range(2):
        inner, corner = ready[s]
        mine = [targets(own, b, (-1.0, float(s - b), 0.0)) for b in range(2)]
        diagonal = targets(outer, s, (-1.0, 1.0 - 2.0 * s, 0.0))
        for r in range(0, BOX, ROWS):
            theirs = sources(columns, s, r)
            along = [t - m for t, m in zip(theirs, diagonal, strict=True)]
            strength = strengths(*along, [corner[k * BOX + r : k * BOX + r + ROWS] for k in range(RADIAL)])
            back = [strength * a for a in along]
            for b in range(2):
                along = [t - m for t, m in zip(theirs, mine[b], strict=True)]
                strength = strengths(
                    *along,
                    [inner[k * BOX + r : k * BOX + r + ROWS, b * BOX : (b + 1) * BOX] for k in range(RADIAL)],
                )
                terms = [strength * a for a in along]
                sums[b] = [t + u for t, u in zip(sums[b], terms, strict=True)]
                back = [t + u for t, u in zip(back, terms, strict=True)]
            x, y, z = [jnp.sum(t, axis=1, keepdims=True) * -SCALE for t in back]
            turned[s, r : r + ROWS, :] = jnp.where(lane == 0, x, jnp.where(lane == 1, y, z))
    for c in range(3):
        forces_ref[c] = so_far_ref[c] + jnp.concatenate([total(sums[0][c]), total(sums[1][c])], axis=0)
    backs = [jnp.transpose(turned[s]) for s in range(2)]
    for c in range(3):
        back_ref[c] = jnp.concatenate([backs[s][c : c + 1] for s in range(2)], axis=0)


def outer_pairs(own_ref, outer_ref, weights_ref, shift):
    rows, columns = rows_of(own_ref), columns_of(outer_ref)
    sums = []
    for s in range(2):
        product = lax.dot_general(box_of(outer_ref, s), weights_ref[s], NN, preferred_element_type=F32)
        mine = targets(rows, s, (shift, 2.0 * s - 1.0, 0.0))
        t = zeros()
        for r in range(0, BOX, ROWS):
            along = [u - m for u, m in zip(sources(columns, s, r), mine, strict=True)]
            strength = strengths(*along, tile(product, r))
            t = [u + strength * a for u, a in zip(t, along, strict=True)]
        sums.append(t)
    return [jnp.concatenate([total(sums[0][c]), total(sums[1][c])], axis=0) for c in range(3)]


def column(own_ref, outer_ref, weights_ref, forces_ref):
    near, far = within(own_ref, weights_ref), outer_pairs(own_ref, outer_ref, weights_ref, 0.0)
    for c in range(3):
        forces_ref[c] = near[c] + far[c]


def corner(own_ref, outer_ref, weights_ref, so_far_ref, forces_ref):
    added = outer_pairs(own_ref, outer_ref, weights_ref, -1.0)
    for c in range(3):
        forces_ref[c] = so_far_ref[c] + added[c]


def finish(so_far_ref, returned_ref, forces_ref):
    forces_ref[...] = so_far_ref[...] + returned_ref[...]


def swap(x, axis, later):
    n = lax.axis_size(axis)
    if later:
        perm = [(i, (i + 1) % n if i % 2 else (i - 1) % n) for i in range(n)]
    else:
        perm = [(i, i + 1 - 2 * (i % 2)) for i in range(n)]
    return lax.ppermute(x, axis, perm)


def pass_on(x, axis, step):
    n = lax.axis_size(axis)
    return lax.ppermute(x, axis, [(i, (i + step) % n) for i in range(n)])


def kernel(body, name, out_shape, n_in, pair_count=0, scratch_shapes=()):
    return pl.pallas_call(
        body,
        out_shape=out_shape,
        in_specs=[vmem()] * n_in,
        out_specs=jax.tree.map(lambda _: vmem(), out_shape),
        scratch_shapes=list(scratch_shapes),
        compiler_params=params(40),
        cost_estimate=pl.CostEstimate(flops=pair_count * 2**27, bytes_accessed=2**18, transcendentals=0),
        name=name,
    )


def on_device(offsets, features, cotangent, w_in, w_out, w_filter, counts):
    turned = jnp.transpose(offsets[0], (1, 0, 2))
    forces_shape = shape(3, 2, BOX)
    own, first, second, filters = pl.pallas_call(
        prepare,
        out_shape=(
            shape(2 * BOX + TAIL, 2 * F, dtype=BF16),
            shape(BOX + TAIL, 2 * F, dtype=BF16),
            shape(BOX + TAIL, 2 * F, dtype=BF16),
            shape(RADIAL, F, dtype=BF16),
        ),
        in_specs=[hbm()] * 7,
        out_specs=(vmem(),) * 4,
        scratch_shapes=[
            pltpu.SMEM((1, 2), jnp.int32),
            pltpu.VMEM((3, 2, BOX), BF16),
            pltpu.VMEM((2, BOX, F), BF16),
            pltpu.VMEM((2, BOX, F), BF16),
            pltpu.VMEM((F, F), BF16),
            pltpu.VMEM((F, F), BF16),
            pltpu.SemaphoreType.DMA((7,)),
        ],
        compiler_params=params(16),
        name="prepare",
    )(*[pltpu.with_memory_space_constraint(x, pltpu.HBM) for x in (counts, turned, features[0], cotangent[0], w_in, w_out, w_filter)])
    second = swap(second, "tower", True)
    before = pass_on(own, "plane", 1)
    first = swap(first, "tower", False)
    weights = kernel(spread, "spread", shape(2, 2 * F, RADIAL * BOX, dtype=BF16), 2, 0)(own, filters)
    outer = kernel(join, "join", shape(2 * BOX + TAIL, 2 * F, dtype=BF16), 3)(second, first, weights)
    before_outer = pass_on(outer, "plane", 1)
    forces = kernel(column, "column", forces_shape, 3, 2)(own, outer, weights)
    forces, back = kernel(
        across,
        "across",
        (forces_shape, forces_shape),
        5,
        8,
        [pltpu.VMEM((2, RADIAL * BOX, 2 * F), BF16), pltpu.VMEM((2, BOX, BOX), F32)],
    )(own, outer, before, filters, forces)
    returned = pass_on(back, "plane", -1)
    forces = kernel(corner, "corner", forces_shape, 4, 2)(own, before_outer, weights, forces)
    forces = kernel(finish, "finish", forces_shape, 2)(forces, returned)
    return jnp.transpose(forces, (1, 0, 2))[None]


def solution(mesh):
    placed = (
        P("plane", "tower", None, None),
        P("plane", "tower", None, None),
        P("plane", "tower", None, None),
        P(),
        P(),
        P(),
        P("plane", "tower"),
    )
    return jax.shard_map(
        on_device,
        mesh=mesh,
        in_specs=placed,
        out_specs=P("plane", "tower", None, None),
        check_vma=False,
    )
```

```python
import math

import jax
import jax.numpy as jnp
from jax import lax
from jax.experimental import pallas as pl
from jax.experimental.pallas import tpu as pltpu
from jax.sharding import PartitionSpec as P

PITCH = 12.5
CUTOFF = 5.0
CENTER_STEP = 3.125
GAMMA = 0.2
FORCE_UNIT = 0.005
LOG2E = math.log2(math.e)

BOX = 128
F = 256
RADIAL = 8
MIDDLE = 4
ROWS = 32
TAIL = 8

LENGTH = PITCH / CUTOFF
SPREAD = GAMMA * CENTER_STEP**2
FACTORS = [math.exp(-SPREAD * (k - MIDDLE) ** 2) for k in range(RADIAL)]
OFFSET = 2.0 / CUTOFF**2 / (2.0 * GAMMA * CENTER_STEP)
SCALE = -2.0 * GAMMA * CENTER_STEP * CUTOFF * 2.0 * FORCE_UNIT

NN = (((1,), (0,)), ((), ()))
NT = (((1,), (1,)), ((), ()))
BF16 = jnp.bfloat16
F32 = jnp.float32


def vmem():
    return pl.BlockSpec(memory_space=pltpu.VMEM)


def hbm():
    return pl.BlockSpec(memory_space=pltpu.HBM)


def params(mib):
    return pltpu.CompilerParams(vmem_limit_bytes=mib * 2**20)


def shape(*dims, dtype=F32):
    return jax.ShapeDtypeStruct(dims, dtype)


def packed_offsets(rows):
    tall = jnp.concatenate([rows, jnp.zeros((TAIL - rows.shape[0], BOX), F32)], axis=0)
    wide = jnp.concatenate([tall, jnp.zeros((TAIL, 2 * F - BOX), F32)], axis=1)
    return wide.astype(BF16)


def prepare(
    counts_ref, offsets_ref, features_ref, cotangent_ref, w_in_ref, w_out_ref, w_filter_ref,
    own_ref, first_ref, second_ref, filter_ref,
    counts, offsets_in, features, cotangent, w_in, w_out, sems,
):
    moves = [
        pltpu.make_async_copy(source, target, sems.at[i])
        for i, (source, target) in enumerate(
            [
                (features_ref, features), (w_in_ref, w_in), (cotangent_ref, cotangent), (w_out_ref, w_out),
                (counts_ref, counts), (offsets_ref, offsets_in), (w_filter_ref, filter_ref),
            ]
        )
    ]
    for move in moves:
        move.start()
    odd = lax.rem(lax.axis_index("tower"), 2)
    slots = lax.broadcasted_iota(jnp.int32, (BOX, F), 0)
    for i in (0, 1, 4):
        moves[i].wait()
    for b in range(2):
        values = jnp.dot(features[b], w_in[...], preferred_element_type=F32)
        own_ref[b * BOX : (b + 1) * BOX, :F] = jnp.where(slots < counts[0, b], values, 0.0).astype(BF16)
    for i in (2, 3, 5, 6):
        moves[i].wait()
    for b in range(2):
        grads = lax.dot_general(cotangent[b], w_out[...], NT, preferred_element_type=F32)
        own_ref[b * BOX : (b + 1) * BOX, F:] = jnp.where(slots < counts[0, b], grads, 0.0).astype(BF16)
    offsets = offsets_in[...].astype(F32)
    own_ref[2 * BOX :, :] = packed_offsets(offsets.reshape(6, BOX))
    first_ref[:BOX, :] = own_ref[pl.ds(pl.multiple_of((1 - odd) * BOX, BOX), BOX), :]
    second_ref[:BOX, :] = own_ref[pl.ds(pl.multiple_of(odd * BOX, BOX), BOX), :]
    first_ref[BOX:, :] = packed_offsets(jnp.where(odd == 1, offsets[:, 0], offsets[:, 1]))
    second_ref[BOX:, :] = packed_offsets(jnp.where(odd == 1, offsets[:, 1], offsets[:, 0]))


def join(second_ref, first_ref, weights_ref, outer_ref):
    odd = lax.rem(lax.axis_index("tower"), 2) == 1
    first = first_ref[...].astype(F32)
    second = second_ref[...].astype(F32)
    below = jnp.where(odd, first, second)
    above = jnp.where(odd, second, first)
    outer_ref[:BOX, :] = below[:BOX].astype(BF16)
    outer_ref[BOX : 2 * BOX, :] = above[:BOX].astype(BF16)
    rows = []
    for c in range(3):
        rows += [below[BOX + c : BOX + c + 1, :BOX], above[BOX + c : BOX + c + 1, :BOX]]
    outer_ref[2 * BOX :, :] = packed_offsets(jnp.concatenate(rows, axis=0))


def strengths(dx, dy, dz, a):
    c = jnp.maximum(1.0 - (dx * dx + dy * dy + dz * dz), 0.0)
    h = MIDDLE - RADIAL * c
    middle = jnp.exp2(h * h * (-SPREAD * LOG2E))
    up = jnp.exp2(h * (2.0 * SPREAD * LOG2E))
    down = jnp.exp2(h * (-2.0 * SPREAD * LOG2E))
    s = up * a[7]
    d = s
    p = a[6] + s
    for k in (5, 4):
        s = up * p
        d = up * d + s
        p = a[k] + s
    s = down * a[0]
    e = s
    for k in (1, 2, 3):
        s = down * (a[k] + s)
        e = down * e + s
    p = p + s
    d = d - e
    return (middle * c) * ((h * c + OFFSET) * p - c * d)


def rows_of(ref):
    return ref[2 * BOX :, :BOX].astype(F32) * LENGTH


def columns_of(ref):
    rows = rows_of(ref)
    return jnp.transpose(jnp.concatenate([rows, jnp.zeros((BOX - TAIL, BOX), F32)], axis=0))


def box_of(ref, b):
    return ref[b * BOX : (b + 1) * BOX, :]


def targets(rows, b, shifts):
    return [rows[2 * c + b : 2 * c + b + 1] - shifts[c] * LENGTH for c in range(3)]


def sources(columns, b, r):
    return [jnp.broadcast_to(columns[r : r + ROWS, 2 * c + b : 2 * c + b + 1], (ROWS, BOX)) for c in range(3)]


def zeros():
    return [jnp.zeros((ROWS, BOX), F32) for _ in range(3)]


def tile(product, r):
    return [product[r : r + ROWS, k * BOX : (k + 1) * BOX] for k in range(RADIAL)]


def total(t):
    return jnp.sum(t, axis=0, keepdims=True) * SCALE


def spread(own_ref, w_filter_ref, weights_ref):
    lanes = lax.broadcasted_iota(jnp.int32, (RADIAL, RADIAL * BOX), 1) // BOX
    picks = (lanes == lax.broadcasted_iota(jnp.int32, (RADIAL, RADIAL * BOX), 0)).astype(F32).astype(BF16)
    w = lax.dot_general(w_filter_ref[...], picks, (((0,), (0,)), ((), ())), preferred_element_type=F32)
    turned = [jnp.transpose(box_of(own_ref, b).astype(F32)) for b in range(2)]
    for k in range(RADIAL):
        broad = w[:, k * BOX : (k + 1) * BOX] * FACTORS[k]
        for b, both in enumerate(turned):
            weights_ref[b, :F, k * BOX : (k + 1) * BOX] = (both[F:] * broad).astype(BF16)
            weights_ref[b, F:, k * BOX : (k + 1) * BOX] = (both[:F] * broad).astype(BF16)


def within(own_ref, weights_ref, turned):
    lane = lax.broadcasted_iota(jnp.int32, (ROWS, BOX), 1)
    rows = rows_of(own_ref)
    columns = columns_of(own_ref)
    sums = [zeros(), zeros()]
    for s, b in ((1, 0), (0, 0), (1, 1)):
        product = lax.dot_general(box_of(own_ref, s), weights_ref[b], NN, preferred_element_type=F32)
        mine = targets(rows, b, (0.0, float(s - b), 0.0))
        for r in range(0, BOX, ROWS):
            along = [t - m for t, m in zip(sources(columns, s, r), mine, strict=True)]
            strength = strengths(*along, tile(product, r))
            terms = [strength * a for a in along]
            sums[b] = [t + u for t, u in zip(sums[b], terms, strict=True)]
            if s != b:
                x, y, z = [jnp.sum(t, axis=1, keepdims=True) * -SCALE for t in terms]
                turned[r : r + ROWS, :] = jnp.where(lane == 0, x, jnp.where(lane == 1, y, z))
    back = jnp.transpose(turned[...])
    return [
        jnp.concatenate([total(sums[0][c]), total(sums[1][c]) + back[c : c + 1]], axis=0) for c in range(3)
    ]


def across(own_ref, outer_ref, before_ref, w_filter_ref, so_far_ref, forces_ref, back_ref, filtered, turned):
    lane = lax.broadcasted_iota(jnp.int32, (ROWS, BOX), 1)
    own, outer, columns = rows_of(own_ref), rows_of(outer_ref), columns_of(before_ref)
    sums = [zeros(), zeros()]
    ready = []
    for s in range(2):
        wide = box_of(before_ref, s).astype(F32)
        for k in range(RADIAL):
            w = w_filter_ref[k : k + 1, :].astype(F32) * FACTORS[k]
            filtered[s, k * BOX : (k + 1) * BOX, :F] = (wide[:, F:] * w).astype(BF16)
            filtered[s, k * BOX : (k + 1) * BOX, F:] = (wide[:, :F] * w).astype(BF16)
        inner = lax.dot_general(filtered[s], own_ref[: 2 * BOX, :], NT, preferred_element_type=F32)
        corner = lax.dot_general(filtered[s], box_of(outer_ref, s), NT, preferred_element_type=F32)
        ready.append((inner, corner))
    for s in range(2):
        inner, corner = ready[s]
        mine = [targets(own, b, (-1.0, float(s - b), 0.0)) for b in range(2)]
        diagonal = targets(outer, s, (-1.0, 1.0 - 2.0 * s, 0.0))
        for r in range(0, BOX, ROWS):
            theirs = sources(columns, s, r)
            along = [t - m for t, m in zip(theirs, diagonal, strict=True)]
            strength = strengths(*along, [corner[k * BOX + r : k * BOX + r + ROWS] for k in range(RADIAL)])
            back = [strength * a for a in along]
            for b in range(2):
                along = [t - m for t, m in zip(theirs, mine[b], strict=True)]
                strength = strengths(
                    *along,
                    [inner[k * BOX + r : k * BOX + r + ROWS, b * BOX : (b + 1) * BOX] for k in range(RADIAL)],
                )
                terms = [strength * a for a in along]
                sums[b] = [t + u for t, u in zip(sums[b], terms, strict=True)]
                back = [t + u for t, u in zip(back, terms, strict=True)]
            x, y, z = [jnp.sum(t, axis=1, keepdims=True) * -SCALE for t in back]
            turned[s, r : r + ROWS, :] = jnp.where(lane == 0, x, jnp.where(lane == 1, y, z))
    for c in range(3):
        forces_ref[c] = so_far_ref[c] + jnp.concatenate([total(sums[0][c]), total(sums[1][c])], axis=0)
    backs = [jnp.transpose(turned[s]) for s in range(2)]
    for c in range(3):
        back_ref[c] = jnp.concatenate([backs[s][c : c + 1] for s in range(2)], axis=0)


def outer_pairs(own_ref, outer_ref, weights_ref, shift):
    rows, columns = rows_of(own_ref), columns_of(outer_ref)
    sums = []
    for s in range(2):
        product = lax.dot_general(box_of(outer_ref, s), weights_ref[s], NN, preferred_element_type=F32)
        mine = targets(rows, s, (shift, 2.0 * s - 1.0, 0.0))
        t = zeros()
        for r in range(0, BOX, ROWS):
            along = [u - m for u, m in zip(sources(columns, s, r), mine, strict=True)]
            strength = strengths(*along, tile(product, r))
            t = [u + strength * a for u, a in zip(t, along, strict=True)]
        sums.append(t)
    return [jnp.concatenate([total(sums[0][c]), total(sums[1][c])], axis=0) for c in range(3)]


def column(own_ref, outer_ref, weights_ref, forces_ref, turned):
    near, far = within(own_ref, weights_ref, turned), outer_pairs(own_ref, outer_ref, weights_ref, 0.0)
    for c in range(3):
        forces_ref[c] = near[c] + far[c]


def corner(own_ref, outer_ref, weights_ref, so_far_ref, forces_ref):
    added = outer_pairs(own_ref, outer_ref, weights_ref, -1.0)
    for c in range(3):
        forces_ref[c] = so_far_ref[c] + added[c]


def finish(so_far_ref, returned_ref, forces_ref):
    forces_ref[...] = so_far_ref[...] + returned_ref[...]


def swap(x, axis, later):
    n = lax.axis_size(axis)
    if later:
        perm = [(i, (i + 1) % n if i % 2 else (i - 1) % n) for i in range(n)]
    else:
        perm = [(i, i + 1 - 2 * (i % 2)) for i in range(n)]
    return lax.ppermute(x, axis, perm)


def pass_on(x, axis, step):
    n = lax.axis_size(axis)
    return lax.ppermute(x, axis, [(i, (i + step) % n) for i in range(n)])


def kernel(body, name, out_shape, n_in, pair_count=0, scratch_shapes=()):
    return pl.pallas_call(
        body,
        out_shape=out_shape,
        in_specs=[vmem()] * n_in,
        out_specs=jax.tree.map(lambda _: vmem(), out_shape),
        scratch_shapes=list(scratch_shapes),
        compiler_params=params(40),
        cost_estimate=pl.CostEstimate(flops=pair_count * 2**27, bytes_accessed=2**18, transcendentals=0),
        name=name,
    )


def on_device(offsets, features, cotangent, w_in, w_out, w_filter, counts):
    turned = jnp.transpose(offsets[0], (1, 0, 2))
    forces_shape = shape(3, 2, BOX)
    own, first, second, filters = pl.pallas_call(
        prepare,
        out_shape=(
            shape(2 * BOX + TAIL, 2 * F, dtype=BF16),
            shape(BOX + TAIL, 2 * F, dtype=BF16),
            shape(BOX + TAIL, 2 * F, dtype=BF16),
            shape(RADIAL, F, dtype=BF16),
        ),
        in_specs=[hbm()] * 7,
        out_specs=(vmem(),) * 4,
        scratch_shapes=[
            pltpu.SMEM((1, 2), jnp.int32),
            pltpu.VMEM((3, 2, BOX), BF16),
            pltpu.VMEM((2, BOX, F), BF16),
            pltpu.VMEM((2, BOX, F), BF16),
            pltpu.VMEM((F, F), BF16),
            pltpu.VMEM((F, F), BF16),
            pltpu.SemaphoreType.DMA((7,)),
        ],
        compiler_params=params(16),
        name="prepare",
    )(*[pltpu.with_memory_space_constraint(x, pltpu.HBM) for x in (counts, turned, features[0], cotangent[0], w_in, w_out, w_filter)])
    second = swap(second, "tower", True)
    before = pass_on(own, "plane", 1)
    first = swap(first, "tower", False)
    weights = kernel(spread, "spread", shape(2, 2 * F, RADIAL * BOX, dtype=BF16), 2, 0)(own, filters)
    outer = kernel(join, "join", shape(2 * BOX + TAIL, 2 * F, dtype=BF16), 3)(second, first, weights)
    before_outer = pass_on(outer, "plane", 1)
    forces = kernel(column, "column", forces_shape, 3, 2, [pltpu.VMEM((BOX, BOX), F32)])(own, outer, weights)
    forces, back = kernel(
        across,
        "across",
        (forces_shape, forces_shape),
        5,
        8,
        [pltpu.VMEM((2, RADIAL * BOX, 2 * F), BF16), pltpu.VMEM((2, BOX, BOX), F32)],
    )(own, outer, before, filters, forces)
    returned = pass_on(back, "plane", -1)
    forces = kernel(corner, "corner", forces_shape, 4, 2)(own, before_outer, weights, forces)
    forces = kernel(finish, "finish", forces_shape, 2)(forces, returned)
    return jnp.transpose(forces, (1, 0, 2))[None]


def solution(mesh):
    placed = (
        P("plane", "tower", None, None),
        P("plane", "tower", None, None),
        P("plane", "tower", None, None),
        P(),
        P(),
        P(),
        P("plane", "tower"),
    )
    return jax.shard_map(
        on_device,
        mesh=mesh,
        in_specs=placed,
        out_specs=P("plane", "tower", None, None),
        check_vma=False,
    )
```
